32 devices in a mesh: shift: 4 (over y, x), rows: 8 (over z, core).
Axes of the slice: x: 2, y: 2, z: 4, core: 2. Of those that a mesh axis runs over, the one named last changes fastest.
Arguments:
- zc_in: bfloat16 [4, 512, 16384], P('shift', 'rows'), may hold values from -6 to 6
- zo_in: bfloat16 [4, 384, 16384], P('shift', 'rows'), may hold values from -6 to 6
- count_c: int32 [4], replicated, may hold values from 256 to 512, as said below
- count_o: int32 [4], replicated, may hold values from 192 to 384, as said below
- mass: bfloat16 [128, 4, 128, 128], P(('shift', 'rows')), may hold values from -0.25 to 0.25
- adjacency: int32 [128, 4], P(('shift', 'rows')), may hold values from 0 to 127, as said below
- ghost_len: int32 [128, 4], P(('shift', 'rows')), may hold values from 1 to 128, as said below
- omega: float32 [2048, 128], replicated, may hold values from -6 to 6
Outputs:
- proj_c: float32 [128, 16384], P(None, ('shift', 'rows'))
- proj_o: float32 [128, 16384], P(None, ('shift', 'rows'))
The draws below stay inside these ranges and needn't reach their ends.
Inputs may be any that keep to these rules, and one draw needn't show every extreme that they name: `count_c`: each entry is 256 or more, and one group holds 512 exactly. `count_o`: each entry is 192 or more, and one group holds 384 exactly. adjacency[i, 0] = i, and every entry lies within 2 blocks of i. ghost_len[i, 0] = 128.
All inputs are finite; a program needn't handle non-finite values.
Results may differ from the reference program's by a relative error of at most 0.0047.
Values may be sent and summed in bfloat16 or wider, within the bound.
A program may use at most 128 MiB of HBM per device.

```python
import jax
import jax.numpy as jnp
from jax import lax

BLOCK_ROWS = 128
NEIGHBORS = 4
REACH = 2
SLOTS_C = 512
SLOTS_O = 384
SKETCH = 128
COLS_C = 2048
BLOCKS = 128
ROWS = 16384
N_SHIFT = 4


def capped_counts(key, most):
    first, second = jax.random.split(key)
    counts = jax.random.randint(first, (N_SHIFT,), most // 2, most + 1)
    full = jax.random.randint(second, (), 0, N_SHIFT)
    return jnp.where(jnp.arange(N_SHIFT) == full, most, counts).astype(jnp.int32)


def draw_count_c(key, part):
    return capped_counts(jax.random.fold_in(key, 11), SLOTS_C)


def draw_count_o(key, part):
    return capped_counts(jax.random.fold_in(key, 23), SLOTS_O)


def draw_adjacency(key, part):
    offsets = jax.random.randint(jax.random.fold_in(key, 37), (BLOCKS, NEIGHBORS), -REACH, REACH + 1)
    column = jnp.arange(NEIGHBORS)[None, :]
    offsets = jnp.where(column == 0, 0, offsets)
    target = jnp.arange(BLOCKS)[:, None] + offsets
    return jnp.clip(target, 0, BLOCKS - 1).astype(jnp.int32)


def draw_ghost_len(key, part):
    lengths = jax.random.randint(jax.random.fold_in(key, 53), (BLOCKS, NEIGHBORS), 1, BLOCK_ROWS + 1)
    column = jnp.arange(NEIGHBORS)[None, :]
    return jnp.where(column == 0, BLOCK_ROWS, lengths).astype(jnp.int32)


def block_scale(stream_key, shape, cuts, least, top_value):
    def one(position, shards_of):
        heights = jax.random.uniform(jax.random.fold_in(jax.random.fold_in(stream_key, 6), position), (shards_of,), jnp.float32, least / len(cuts), top_value / len(cuts))
        return jnp.repeat(jnp.exp(heights), shape[position] // shards_of).reshape((-1,) + (1,) * (len(shape) - position - 1))

    level = one(*cuts[0])
    for cut in cuts[1:]:
        level = level * one(*cut)
    return level


def gaussian(key, dims, width, most, shards=(), kind=jnp.bfloat16):
    level = block_scale(key, dims, shards, -0.22, 0.18) if shards else 1.0
    values = jax.random.normal(key, dims, jnp.float32) * width * level
    return jnp.minimum(jnp.maximum(values, -most), most).astype(kind)


def setup_inputs(seed: int = 0) -> dict:
    keys = jax.random.split(jax.random.key(seed), 9)
    zc_in = gaussian(keys[0], (N_SHIFT, SLOTS_C, ROWS), 1.0, 6.0, ((0, 4), (1, 8)))
    zo_in = gaussian(keys[1], (N_SHIFT, SLOTS_O, ROWS), 1.0, 6.0, ((0, 4), (1, 8)))
    count_c = draw_count_c(jax.random.fold_in(keys[8], 71), 0)
    count_o = draw_count_o(jax.random.fold_in(keys[8], 71), 0)
    mass = gaussian(keys[4], (BLOCKS, NEIGHBORS, BLOCK_ROWS, BLOCK_ROWS), (NEIGHBORS * BLOCK_ROWS) ** -0.5, 0.25, ((0, 32),))
    adjacency = draw_adjacency(jax.random.fold_in(keys[8], 71), 0)
    ghost_len = draw_ghost_len(jax.random.fold_in(keys[8], 71), 0)
    omega = gaussian(keys[7], (COLS_C, SKETCH), 1.0, 6.0, (), jnp.float32)
    return {"zc_in": zc_in, "zo_in": zo_in, "count_c": count_c, "count_o": count_o, "mass": mass, "adjacency": adjacency, "ghost_len": ghost_len, "omega": omega}


def masked_factor(factor, counts):
    slots = jnp.arange(factor.shape[1], dtype=jnp.int32)[None, :, None]
    keep = slots < counts[:, None, None]
    return jnp.where(keep, factor, jnp.zeros_like(factor)).reshape(-1, factor.shape[2])

def orth(matrix):
    square = jnp.dot(matrix.T, matrix, precision=lax.Precision.HIGHEST)
    lower = jnp.linalg.cholesky(square)
    return jax.scipy.linalg.solve_triangular(lower, matrix.T, lower=True).T

def reference(zc_in, zo_in, count_c, count_o, mass, adjacency, ghost_len, omega):
    zc = masked_factor(zc_in, count_c)
    zo = masked_factor(zo_in, count_o)
    inner = jnp.arange(BLOCK_ROWS, dtype=jnp.int32)
    keep = inner[None, None, None, :] < ghost_len[:, :, None, None]
    masked = jnp.where(keep, mass, jnp.zeros_like(mass))
    blocks = zc.reshape(COLS_C, BLOCKS, BLOCK_ROWS)

    def apply_row(index):
        pieces = jnp.take(blocks, adjacency[index], axis=1).astype(jnp.float32)
        local = masked[index].astype(jnp.float32)
        return jnp.einsum('ckp,kqp->cq', pieces, local).astype(jnp.bfloat16)
    mixed = lax.map(apply_row, jnp.arange(BLOCKS, dtype=jnp.int32))
    mixed = jnp.transpose(mixed, (1, 0, 2)).reshape(COLS_C, ROWS)
    gram = lax.dot_general(zo.astype(jnp.float32), mixed.astype(jnp.float32), (((1,), (1,)), ((), ())), preferred_element_type=jnp.float32)
    high = lax.Precision.HIGHEST
    first = orth(jnp.dot(gram, omega, precision=high))
    right = orth(jnp.dot(gram.T, first, precision=high))
    left = orth(jnp.dot(gram, right, precision=high))
    proj_c = jnp.dot(right.astype(jnp.bfloat16).T.astype(jnp.float32), zc.astype(jnp.float32), preferred_element_type=jnp.float32)
    proj_o = jnp.dot(left.astype(jnp.bfloat16).T.astype(jnp.float32), zo.astype(jnp.float32), preferred_element_type=jnp.float32)
    return (proj_c, proj_o)
```

```python
import jax
import jax.numpy as jnp
from jax import lax
from jax.sharding import PartitionSpec as P

REACH = 2
AXES = ("shift", "rows")
F32 = jnp.float32
BF16 = jnp.bfloat16


def split(matrix):
    high = lax.reduce_precision(matrix, 8, 7)
    return jnp.concatenate([high.astype(BF16), (matrix - high).astype(BF16)], axis=-1)


def joined(matrix):
    half = matrix.shape[-1] // 2
    return matrix[..., :half] + matrix[..., half:]


def dot(left, right, contract_left, contract_right):
    return lax.dot_general(
        left, right, (((contract_left,), (contract_right,)), ((), ())), preferred_element_type=F32
    )


def live(counts, slots):
    inner = jnp.arange(slots, dtype=jnp.int32)
    return (inner[None, :] < counts[:, None]).reshape(-1, 1)


def orth_local(matrix):
    square = jnp.dot(matrix.T, matrix, precision=lax.Precision.HIGHEST)
    lower = jnp.linalg.cholesky(square)
    return jax.scipy.linalg.solve_triangular(lower, matrix.T, lower=True).T


def per_device(zc_in, zo_in, count_c, count_o, mass, adjacency, ghost_len, omega):
    index = lax.axis_index(AXES)
    devices = lax.axis_size(AXES)
    zc = lax.all_to_all(zc_in[0], AXES, split_axis=1, concat_axis=0, tiled=True)
    zo = lax.all_to_all(zo_in[0], AXES, split_axis=1, concat_axis=0, tiled=True)
    groups = count_c.shape[0]
    live_c = live(count_c, zc.shape[0] // groups)
    live_o = live(count_o, zo.shape[0] // groups)
    size = mass.shape[2]
    count, near = adjacency.shape
    local = adjacency - index * count + REACH
    inner = jnp.arange(size, dtype=jnp.int32)
    masked = jnp.where(inner < ghost_len[:, :, None, None], mass, jnp.zeros_like(mass))
    places = jnp.arange(count + 2 * REACH, dtype=jnp.int32)
    hit = (local[:, :, None] == places)[:, :, None, :, None]
    dense = jnp.where(hit, masked[:, :, :, None, :].astype(F32), 0.0).sum(axis=1)
    dense = dense.reshape(count * size, -1)
    banded = lax.reduce_precision(dense, 8, 7)
    banded_rest = (dense - banded).astype(BF16)
    banded = banded.astype(BF16)
    up = [(i, i + 1) for i in range(devices - 1)]
    down = [(j, i) for i, j in up]
    edge = REACH * size
    width = omega.shape[1]

    def forward(right):
        rows = joined(dot(zc, split(right), 0, 0))
        before = lax.ppermute(rows[-edge:], AXES, up)
        after = lax.ppermute(rows[:edge], AXES, down)
        wide = split(jnp.concatenate([before, rows, after], axis=0))
        mixed = joined(dot(banded, wide, 1, 0) + dot(banded_rest, wide, 1, 0))
        part = joined(dot(zo, split(mixed), 1, 0))
        return jnp.where(live_o, lax.psum(part, AXES), 0.0)

    def backward(left):
        rows = dot(zo, split(left), 0, 0)
        rows = split(joined(rows))
        wide = joined(dot(banded, rows, 0, 0) + dot(banded_rest, rows, 0, 0))
        above = lax.ppermute(wide[-edge:], AXES, up)
        below = lax.ppermute(wide[:edge], AXES, down)
        rows = wide[edge:-edge]
        rows = rows + jnp.pad(above, ((0, rows.shape[0] - edge), (0, 0)))
        rows = rows + jnp.pad(below, ((rows.shape[0] - edge, 0), (0, 0)))
        part = joined(dot(zc, split(rows), 1, 0))
        return jnp.where(live_c, lax.psum(part, AXES), 0.0)

    first = orth_local(forward(jnp.where(live_c, omega, 0.0)))
    right = orth_local(backward(first))
    proj_c = dot(right.astype(BF16), zc, 0, 0)
    left = orth_local(forward(right))
    proj_o = dot(left.astype(BF16), zo, 0, 0)
    return (proj_c, proj_o)


def solution(mesh):
    placed = (
        P("shift", "rows", None),
        P("shift", "rows", None),
        P(),
        P(),
        P(AXES, None, None, None),
        P(AXES, None),
        P(AXES, None),
        P(),
    )
    return jax.shard_map(
        per_device,
        mesh=mesh,
        in_specs=placed,
        out_specs=(P(None, AXES), P(None, AXES)),
        check_vma=False,
    )
```

```python
import functools

import jax
import jax.numpy as jnp
from jax import lax
from jax.experimental import pallas as pl
from jax.experimental.pallas import tpu as pltpu
from jax.sharding import PartitionSpec as P

REACH = 2
AXES = ("shift", "rows")
F32 = jnp.float32
BF16 = jnp.bfloat16


def split(matrix):
    high = lax.reduce_precision(matrix, 8, 7)
    return jnp.concatenate([high.astype(BF16), (matrix - high).astype(BF16)], axis=-1)


def joined(matrix):
    half = matrix.shape[-1] // 2
    return matrix[..., :half] + matrix[..., half:]


def dot(left, right, contract_left, contract_right):
    return lax.dot_general(
        left, right, (((contract_left,), (contract_right,)), ((), ())), preferred_element_type=F32
    )


def live(counts, slots):
    inner = jnp.arange(slots, dtype=jnp.int32)
    return (inner[None, :] < counts[:, None]).reshape(-1, 1)


MESH = pl.DeviceIdType.MESH


def sum_kernel(shifts, members, part_ref, out_ref, total, landing, send_sem, recv_sem):
    group = lax.axis_index("shift")
    member = lax.axis_index("rows")
    pairs = members // 2
    core = lax.rem(member, 2)
    pair = member // 2

    def core_peer(step):
        return (group, pair * 2 + lax.rem(core + step, 2))

    def shift_peer(step):
        return (lax.rem(group + step, shifts), member)

    def pair_peer(step):
        return (group, lax.rem(pair + step, pairs) * 2 + core)

    stages = [(2, core, core_peer), (shifts, group, shift_peer), (pairs, pair, pair_peer)]
    stages = [stage for stage in stages if stage[0] > 1]

    barrier = pltpu.get_barrier_semaphore()
    peers = 0
    for size, _, peer in stages:
        for step in range(1, size):
            pl.semaphore_signal(barrier, inc=1, device_id=peer(step), device_id_type=MESH)
            peers += 1
    pl.semaphore_wait(barrier, peers)

    rows = part_ref.shape[0]
    length = rows
    start = 0
    used = 0
    place = 0
    source = part_ref
    spans = []
    for size, position, peer in stages:
        piece = length // size
        copies = []
        for step in range(1, size):
            target = start + lax.rem(position + step, size) * piece
            copy = pltpu.make_async_remote_copy(
                src_ref=source.at[pl.ds(pl.multiple_of(target, 8), piece)],
                dst_ref=landing.at[pl.ds(place + (step - 1) * piece, piece)],
                send_sem=send_sem.at[used],
                recv_sem=recv_sem.at[used],
                device_id=peer(step),
                device_id_type=MESH,
            )
            copy.start()
            copies.append(copy)
            used += 1
        start = start + position * piece
        mine = pl.ds(pl.multiple_of(start, 8), piece)
        for copy in copies:
            copy.wait()
        value = source[mine]
        for step in range(1, size):
            value = value + landing[pl.ds(place + (step - 1) * piece, piece)]
        length = piece
        place += (size - 1) * piece
        spans.append((mine, size, peer))
        if len(spans) == len(stages):
            out_ref[mine] = value
        else:
            total[mine] = value
            source = total
    for mine, size, peer in reversed(spans):
        copies = []
        for step in range(1, size):
            copy = pltpu.make_async_remote_copy(
                src_ref=out_ref.at[mine],
                dst_ref=out_ref.at[mine],
                send_sem=send_sem.at[used],
                recv_sem=recv_sem.at[used],
                device_id=peer(step),
                device_id_type=MESH,
            )
            copy.start()
            copies.append(copy)
            used += 1
        for copy in copies:
            copy.wait()


def summed(part, call):
    shifts, members = lax.axis_size("shift"), lax.axis_size("rows")
    rows = part.shape[0]
    step = 8 * shifts * members
    padded = -(-rows // step) * step
    if padded > rows:
        part = jnp.pad(part, ((0, padded - rows), (0, 0)))
    copies = 2 * (1 + shifts - 1 + members // 2 - 1)
    total = pl.pallas_call(
        functools.partial(sum_kernel, shifts, members),
        out_shape=jax.ShapeDtypeStruct(part.shape, F32),
        in_specs=[pl.BlockSpec(memory_space=pltpu.VMEM)],
        out_specs=pl.BlockSpec(memory_space=pltpu.VMEM),
        scratch_shapes=[
            pltpu.VMEM(part.shape, F32),
            pltpu.VMEM(part.shape, F32),
            pltpu.SemaphoreType.DMA((copies,)),
            pltpu.SemaphoreType.DMA((copies,)),
        ],
        compiler_params=pltpu.CompilerParams(collective_id=call, has_side_effects=True),
        name="summed%d" % call,
    )(part)
    return total[:rows]


def orth_local(matrix):
    square = jnp.dot(matrix.T, matrix, precision=lax.Precision.HIGHEST)
    lower = jnp.linalg.cholesky(square)
    return jax.scipy.linalg.solve_triangular(lower, matrix.T, lower=True).T


def per_device(zc_in, zo_in, count_c, count_o, mass, adjacency, ghost_len, omega):
    index = lax.axis_index(AXES)
    devices = lax.axis_size(AXES)
    zc = lax.all_to_all(zc_in[0], AXES, split_axis=1, concat_axis=0, tiled=True)
    zo = lax.all_to_all(zo_in[0], AXES, split_axis=1, concat_axis=0, tiled=True)
    groups = count_c.shape[0]
    live_c = live(count_c, zc.shape[0] // groups)
    live_o = live(count_o, zo.shape[0] // groups)
    size = mass.shape[2]
    count, near = adjacency.shape
    local = adjacency - index * count + REACH
    inner = jnp.arange(size, dtype=jnp.int32)
    masked = jnp.where(inner < ghost_len[:, :, None, None], mass, jnp.zeros_like(mass))
    places = jnp.arange(count + 2 * REACH, dtype=jnp.int32)
    hit = (local[:, :, None] == places)[:, :, None, :, None]
    dense = jnp.where(hit, masked[:, :, :, None, :].astype(F32), 0.0).sum(axis=1)
    dense = dense.reshape(count * size, -1)
    banded = lax.reduce_precision(dense, 8, 7)
    banded_rest = (dense - banded).astype(BF16)
    banded = banded.astype(BF16)
    up = [(i, i + 1) for i in range(devices - 1)]
    down = [(j, i) for i, j in up]
    edge = REACH * size
    width = omega.shape[1]

    def forward(right, call):
        rows = joined(dot(zc, split(right), 0, 0))
        before = lax.ppermute(rows[-edge:], AXES, up)
        after = lax.ppermute(rows[:edge], AXES, down)
        wide = split(jnp.concatenate([before, rows, after], axis=0))
        mixed = joined(dot(banded, wide, 1, 0) + dot(banded_rest, wide, 1, 0))
        part = joined(dot(zo, split(mixed), 1, 0))
        return jnp.where(live_o, summed(part, call), 0.0)

    def backward(left, call):
        rows = dot(zo, split(left), 0, 0)
        rows = split(joined(rows))
        wide = joined(dot(banded, rows, 0, 0) + dot(banded_rest, rows, 0, 0))
        above = lax.ppermute(wide[-edge:], AXES, up)
        below = lax.ppermute(wide[:edge], AXES, down)
        rows = wide[edge:-edge]
        rows = rows + jnp.pad(above, ((0, rows.shape[0] - edge), (0, 0)))
        rows = rows + jnp.pad(below, ((rows.shape[0] - edge, 0), (0, 0)))
        part = joined(dot(zc, split(rows), 1, 0))
        return jnp.where(live_c, summed(part, call), 0.0)

    first = orth_local(forward(jnp.where(live_c, omega, 0.0), 0))
    right = orth_local(backward(first, 1))
    proj_c = dot(right.astype(BF16), zc, 0, 0)
    left = orth_local(forward(right, 2))
    proj_o = dot(left.astype(BF16), zo, 0, 0)
    return (proj_c, proj_o)


def solution(mesh):
    placed = (
        P("shift", "rows", None),
        P("shift", "rows", None),
        P(),
        P(),
        P(AXES, None, None, None),
        P(AXES, None),
        P(AXES, None),
        P(),
    )
    return jax.shard_map(
        per_device,
        mesh=mesh,
        in_specs=placed,
        out_specs=(P(None, AXES), P(None, AXES)),
        check_vma=False,
    )
```

```python
import functools

import jax
import jax.numpy as jnp
from jax import lax
from jax.experimental import pallas as pl
from jax.experimental.pallas import tpu as pltpu
from jax.sharding import PartitionSpec as P

REACH = 2
AXES = ("shift", "rows")
F32 = jnp.float32
BF16 = jnp.bfloat16


def split(matrix):
    high = lax.reduce_precision(matrix, 8, 7)
    return jnp.concatenate([high.astype(BF16), (matrix - high).astype(BF16)], axis=-1)


def joined(matrix):
    half = matrix.shape[-1] // 2
    return matrix[..., :half] + matrix[..., half:]


def dot(left, right, contract_left, contract_right):
    return lax.dot_general(
        left, right, (((contract_left,), (contract_right,)), ((), ())), preferred_element_type=F32
    )


def live(counts, slots):
    inner = jnp.arange(slots, dtype=jnp.int32)
    return (inner[None, :] < counts[:, None]).reshape(-1, 1)


MESH = pl.DeviceIdType.MESH


def halved(matrix):
    high = matrix.astype(BF16)
    return high, (matrix - high.astype(F32)).astype(BF16)


def times(left, right):
    high, rest = halved(right)
    return dot(left, high, 1, 0) + dot(left, rest, 1, 0)


def sum_kernel(shifts, members, kind, edge, rows_ref, *refs):
    if kind == "forward":
        banded_ref, rest_ref, factor_ref, live_ref = refs[:4]
    else:
        factor_ref, live_ref = refs[:2]
    out_ref, part_ref, total, landing, halo, send_sem, recv_sem, halo_send, halo_recv = refs[-9:]
    group = lax.axis_index("shift")
    member = lax.axis_index("rows")
    pairs = members // 2
    devices = shifts * members
    index = group * members + member
    sides = []
    for step in (1, devices - 1):
        beside = lax.rem(index + step, devices)
        sides.append((beside // members, lax.rem(beside, members)))
    core = lax.rem(member, 2)
    pair = member // 2

    def core_peer(step):
        return (group, pair * 2 + lax.rem(core + step, 2))

    def shift_peer(step):
        return (lax.rem(group + step, shifts), member)

    def pair_peer(step):
        return (group, lax.rem(pair + step, pairs) * 2 + core)

    stages = [(2, core, core_peer), (shifts, group, shift_peer), (pairs, pair, pair_peer)]
    stages = [stage for stage in stages if stage[0] > 1]

    barrier = pltpu.get_barrier_semaphore()
    peers = 0
    for size, _, peer in stages:
        for step in range(1, size):
            pl.semaphore_signal(barrier, inc=1, device_id=peer(step), device_id_type=MESH)
            peers += 1
    for side in sides:
        pl.semaphore_signal(barrier, inc=1, device_id=side, device_id_type=MESH)
    pl.semaphore_wait(barrier, peers + 2)

    depth = rows_ref.shape[0]
    halos = []
    for n, first in ((0, depth - edge), (1, 0)):
        copy = pltpu.make_async_remote_copy(
            src_ref=rows_ref.at[pl.ds(first, edge)],
            dst_ref=halo.at[n],
            send_sem=halo_send.at[n],
            recv_sem=halo_recv.at[n],
            device_id=sides[n],
            device_id_type=MESH,
        )
        copy.start()
        halos.append(copy)
    for copy in halos:
        copy.wait()
    if kind == "forward":
        wide = jnp.concatenate([halo[0], rows_ref[...], halo[1]], axis=0)
        mixed = times(banded_ref[...], wide) + times(rest_ref[...], wide)
    else:
        kept = rows_ref[pl.ds(edge, depth - 2 * edge), :]
        blank = jnp.zeros((depth - 3 * edge, kept.shape[1]), F32)
        mixed = kept + jnp.concatenate([halo[0], blank], axis=0)
        mixed = mixed + jnp.concatenate([blank, halo[1]], axis=0)
    count = factor_ref.shape[0]
    part_ref[pl.ds(0, count), :] = times(factor_ref[...], mixed) * live_ref[...]
    if part_ref.shape[0] > count:
        part_ref[pl.ds(count, part_ref.shape[0] - count), :] = jnp.zeros(
            (part_ref.shape[0] - count, part_ref.shape[1]), F32
        )

    rows = part_ref.shape[0]
    length = rows
    start = 0
    used = 0
    place = 0
    source = part_ref
    spans = []
    for size, position, peer in stages:
        piece = length // size
        copies = []
        for step in range(1, size):
            target = start + lax.rem(position + step, size) * piece
            copy = pltpu.make_async_remote_copy(
                src_ref=source.at[pl.ds(pl.multiple_of(target, 8), piece)],
                dst_ref=landing.at[pl.ds(place + (step - 1) * piece, piece)],
                send_sem=send_sem.at[used],
                recv_sem=recv_sem.at[used],
                device_id=peer(step),
                device_id_type=MESH,
            )
            copy.start()
            copies.append(copy)
            used += 1
        start = start + position * piece
        mine = pl.ds(pl.multiple_of(start, 8), piece)
        for copy in copies:
            copy.wait()
        value = source[mine]
        for step in range(1, size):
            value = value + landing[pl.ds(place + (step - 1) * piece, piece)]
        length = piece
        place += (size - 1) * piece
        spans.append((mine, size, peer))
        if len(spans) == len(stages):
            out_ref[mine] = value
        else:
            total[mine] = value
            source = total
    for mine, size, peer in reversed(spans):
        copies = []
        for step in range(1, size):
            copy = pltpu.make_async_remote_copy(
                src_ref=out_ref.at[mine],
                dst_ref=out_ref.at[mine],
                send_sem=send_sem.at[used],
                recv_sem=recv_sem.at[used],
                device_id=peer(step),
                device_id_type=MESH,
            )
            copy.start()
            copies.append(copy)
            used += 1
        for copy in copies:
            copy.wait()


def summed(kind, edge, call, rows, *others):
    shifts, members = lax.axis_size("shift"), lax.axis_size("rows")
    count, width = others[-1].shape[0], rows.shape[1]
    step = 8 * shifts * members
    shape = (-(-count // step) * step, width)
    copies = 2 * (1 + shifts - 1 + members // 2 - 1)
    total = pl.pallas_call(
        functools.partial(sum_kernel, shifts, members, kind, edge),
        out_shape=jax.ShapeDtypeStruct(shape, F32),
        in_specs=[pl.BlockSpec(memory_space=pltpu.VMEM)] * (1 + len(others)),
        out_specs=pl.BlockSpec(memory_space=pltpu.VMEM),
        scratch_shapes=[
            pltpu.VMEM(shape, F32),
            pltpu.VMEM(shape, F32),
            pltpu.VMEM(shape, F32),
            pltpu.VMEM((2, edge, width), F32),
            pltpu.SemaphoreType.DMA((copies,)),
            pltpu.SemaphoreType.DMA((copies,)),
            pltpu.SemaphoreType.DMA((2,)),
            pltpu.SemaphoreType.DMA((2,)),
        ],
        compiler_params=pltpu.CompilerParams(
            collective_id=call, has_side_effects=True, vmem_limit_bytes=40 * 1024 * 1024
        ),
        name="summed%d" % call,
    )(rows, *others)
    return total[:count]


def orth_kernel(matrix_ref, out_ref, square):
    width = matrix_ref.shape[1]
    high = lax.Precision.HIGHEST
    matrix = matrix_ref[...]
    square[...] = lax.dot_general(
        matrix, matrix, (((0,), (0,)), ((), ())), precision=high, preferred_element_type=F32
    )
    lanes = lax.broadcasted_iota(jnp.int32, (8, width), 1)
    below = lax.broadcasted_iota(jnp.int32, (8, width), 0)
    panels = width // 8
    groups = [square[8 * g : 8 * g + 8, :] for g in range(panels)]
    for k in range(panels):
        base = 8 * k
        inside = (lanes >= base) & (lanes < base + 8)
        columns = {
            g: [jnp.broadcast_to(groups[g][:, base + j : base + j + 1], (8, width)) for j in range(8)]
            for g in range(k, panels)
        }
        unit = jnp.where(lanes == below + base, 1.0, 0.0)
        groups[k] = jnp.where(inside, unit, groups[k])
        for g in range(k + 1, panels):
            groups[g] = jnp.where(inside, 0.0, groups[g])
        pivots = jnp.ones((8, width), F32)
        for j in range(8):
            own = columns[k]
            pivot = jnp.broadcast_to(own[j][j : j + 1, :], (8, width))
            inverse = 1.0 / pivot
            pivots = jnp.where(below == j, pivot, pivots)
            row = jnp.broadcast_to(groups[k][j : j + 1, :], (8, width))
            heads = [
                jnp.broadcast_to(own[n][j : j + 1, :], (8, width)) if n > j else None for n in range(8)
            ]
            for g in range(k, panels):
                factor = columns[g][j] * inverse
                if g == k:
                    factor = jnp.where(below > j, factor, 0.0)
                for n in range(j + 1, 8):
                    columns[g][n] = columns[g][n] - factor * heads[n]
                groups[g] = groups[g] - factor * row
        done = jnp.where(lanes < base + 8, groups[k] * lax.rsqrt(pivots), 0.0)
        square[base : base + 8, :] = done
    out_ref[...] = lax.dot_general(
        matrix_ref[...], square[...], (((1,), (1,)), ((), ())), precision=high, preferred_element_type=F32
    )


def orth_local(matrix):
    width = matrix.shape[1]
    return pl.pallas_call(
        orth_kernel,
        out_shape=jax.ShapeDtypeStruct(matrix.shape, F32),
        in_specs=[pl.BlockSpec(memory_space=pltpu.VMEM)],
        out_specs=pl.BlockSpec(memory_space=pltpu.VMEM),
        scratch_shapes=[pltpu.VMEM((width, width), F32)],
        name="orth",
    )(matrix)


def per_device(zc_in, zo_in, count_c, count_o, mass, adjacency, ghost_len, omega):
    index = lax.axis_index(AXES)
    zc = lax.all_to_all(zc_in[0], AXES, split_axis=1, concat_axis=0, tiled=True)
    zo = lax.all_to_all(zo_in[0], AXES, split_axis=1, concat_axis=0, tiled=True)
    groups = count_c.shape[0]
    live_c = live(count_c, zc.shape[0] // groups)
    live_o = live(count_o, zo.shape[0] // groups)
    size = mass.shape[2]
    count, near = adjacency.shape
    local = adjacency - index * count + REACH
    inner = jnp.arange(size, dtype=jnp.int32)
    masked = jnp.where(inner < ghost_len[:, :, None, None], mass, jnp.zeros_like(mass))
    places = jnp.arange(count + 2 * REACH, dtype=jnp.int32)
    hit = (local[:, :, None] == places)[:, :, None, :, None]
    dense = jnp.where(hit, masked[:, :, :, None, :].astype(F32), 0.0).sum(axis=1)
    dense = dense.reshape(count * size, -1)
    banded = lax.reduce_precision(dense, 8, 7)
    banded_rest = (dense - banded).astype(BF16)
    banded = banded.astype(BF16)
    edge = REACH * size

    def forward(right, call):
        rows = joined(dot(zc, split(right), 0, 0))
        return summed("forward", edge, call, rows, banded, banded_rest, zo, live_o.astype(F32))

    def backward(left, call):
        rows = dot(zo, split(left), 0, 0)
        rows = split(joined(rows))
        wide = joined(dot(banded, rows, 0, 0) + dot(banded_rest, rows, 0, 0))
        return summed("backward", edge, call, wide, zc, live_c.astype(F32))

    first = orth_local(forward(jnp.where(live_c, omega, 0.0), 0))
    right = orth_local(backward(first, 1))
    proj_c = dot(right.astype(BF16), zc, 0, 0)
    left = orth_local(forward(right, 2))
    proj_o = dot(left.astype(BF16), zo, 0, 0)
    return (proj_c, proj_o)


def solution(mesh):
    placed = (
        P("shift", "rows", None),
        P("shift", "rows", None),
        P(),
        P(),
        P(AXES, None, None, None),
        P(AXES, None),
        P(AXES, None),
        P(),
    )
    return jax.shard_map(
        per_device,
        mesh=mesh,
        in_specs=placed,
        out_specs=(P(None, AXES), P(None, AXES)),
        check_vma=False,
    )
```
